1024 devices in a mesh: dp: 32 (over z, core), owner: 32 (over x, y).
Axes of the slice: x: 4, y: 8, z: 16, core: 2. Of those that a mesh axis runs over, the one named last changes fastest.
Arguments:
- grad_rows: bfloat16 [262144, 1024], P(('dp', 'owner')), may hold values from -6 to 6
- token_owner: int32 [262144], P(('dp', 'owner')), may hold values from 0 to 31, as said below
- token_slot: int32 [262144], P(('dp', 'owner')), may hold values from 0 to 39
- ngram_input: bfloat16 [40960, 1024], P(('dp', 'owner')), may hold values from -6 to 6
- up_weight: bfloat16 [1024, 4096], P(None, 'dp'), may hold values from -0.1875 to 0.1875
- down_weight: bfloat16 [4096, 1024], P('dp'), may hold values from -0.09375 to 0.09375
Outputs:
- grad_up: float32 [1024, 4096], P('owner', 'dp')
- grad_down: float32 [4096, 1024], P('dp', 'owner')
The draws below stay inside these ranges and needn't reach their ends.
Inputs may be any that keep to these rules, and one draw needn't show every extreme that they name: `token_owner`: from the positions of one device at most 16 go to any one owner; in every data group one owner receives exactly 16 from every device of the group.
All inputs are finite; a program needn't handle non-finite values.
Results may differ from the reference program's by a relative error of at most 0.0041.
Values may be sent and summed in bfloat16 or wider, within the bound.
A program may use at most 32 MiB of HBM per device.

```python
import jax
import jax.numpy as jnp
from jax import lax

D = 1024
FF = 4096
TOK_DEV = 256
NG_DEV = 40
GROUPS = 32
OWNERS = 32
CAP = 16
TOKENS = 262144
NGRAMS = 40960


def draw_token_owner(key, part):
    key = jax.random.fold_in(key, 11)
    key_hot, key_rest = jax.random.split(key)
    hot = jax.random.randint(key_hot, (GROUPS,), 0, OWNERS).astype(jnp.int32)
    labels = (jnp.arange((OWNERS - 1) * CAP, dtype=jnp.int32) // CAP).astype(jnp.int32)
    device_keys = jax.random.split(key_rest, GROUPS * OWNERS)

    def one_device(device_key, chosen):
        key_pick, key_order = jax.random.split(device_key)
        others = jax.random.permutation(key_pick, labels)[:TOK_DEV - CAP]
        marks = jnp.concatenate([jnp.zeros((CAP,), jnp.int32) - 1, others.astype(jnp.int32)])
        peers = (marks + 1 + chosen) % OWNERS
        return jax.random.permutation(key_order, peers).astype(jnp.int32)
    chosen_all = jnp.repeat(hot, OWNERS)
    return jax.vmap(one_device)(device_keys, chosen_all).reshape(TOKENS).astype(jnp.int32)


def place_ends(values, stream_key, low, largest):
    extent = values.shape
    spot = [jax.random.randint(jax.random.fold_in(stream_key, axis), (), 0, extent[axis]) for axis in range(len(extent))]
    values = values.at[tuple(spot)].set(low)
    longest = extent.index(max(extent))
    spot[longest] = (spot[longest] + 1) % extent[longest]
    return values.at[tuple(spot)].set(largest)


def steps_of(stream_key, shape, pieces, low, largest):
    gain = 1.0
    for axis_at, blocks in pieces:
        steps = jax.random.uniform(jax.random.fold_in(jax.random.fold_in(stream_key, 6), axis_at), (blocks,), jnp.float32, low / len(pieces), largest / len(pieces))
        gain = gain * jnp.repeat(jnp.exp(steps), shape[axis_at] // blocks).reshape((-1,) + (1,) * (len(shape) - 1 - axis_at))
    return gain


def noise(stream_key, shape, deviation, limit, shards=(), kind=jnp.bfloat16):
    values = deviation * jax.random.normal(stream_key, shape, jnp.float32)
    if shards:
        values = values * steps_of(stream_key, shape, shards, -0.22, 0.18)
    return jnp.clip(values, -limit, limit).astype(kind)


def setup_inputs(seed: int = 0) -> dict:
    key_list = jax.random.split(jax.random.key(seed), 7)
    grad_rows = noise(key_list[0], (TOKENS, D), 1.0, 6.0, ((0, 1024),))
    token_owner = draw_token_owner(jax.random.fold_in(key_list[6], 71), 0)
    token_slot = place_ends(jax.random.randint(key_list[2], (TOKENS,), 0, NG_DEV), jax.random.fold_in(key_list[2], 1), 0, NG_DEV - 1).astype(jnp.int32)
    ngram_input = noise(key_list[3], (NGRAMS, D), 1.0, 6.0, ((0, 1024),))
    up_weight = noise(key_list[4], (D, FF), D ** -0.5, 0.1875, ((1, 32),))
    down_weight = noise(key_list[5], (FF, D), FF ** -0.5, 0.09375, ((0, 32),))
    return dict(grad_rows=grad_rows, token_owner=token_owner, token_slot=token_slot, ngram_input=ngram_input, up_weight=up_weight, down_weight=down_weight)


def reference(grad_rows, token_owner, token_slot, ngram_input, up_weight, down_weight):
    position = jnp.arange(TOKENS, dtype=jnp.int32)
    group = position // (TOK_DEV * OWNERS)
    target = (group * OWNERS + token_owner) * NG_DEV + token_slot
    summed = jax.ops.segment_sum(grad_rows.astype(jnp.float32), target, num_segments=NGRAMS)
    ngram_grad = summed.astype(jnp.bfloat16)
    block = min(NGRAMS, 2048)
    count = NGRAMS // block

    def step(carry, index):
        inputs = lax.dynamic_slice_in_dim(ngram_input, index * block, block, 0)
        grads = lax.dynamic_slice_in_dim(ngram_grad, index * block, block, 0)
        pre = jnp.dot(inputs, up_weight, preferred_element_type=jnp.float32)
        act = jax.nn.gelu(pre).astype(jnp.bfloat16)
        d_act = lax.dot_general(grads, down_weight, (((1,), (1,)), ((), ())), preferred_element_type=jnp.float32)
        d_pre = jax.vjp(jax.nn.gelu, pre)[1](d_act)[0].astype(jnp.bfloat16)
        upper = carry[0] + lax.dot_general(inputs, d_pre, (((0,), (0,)), ((), ())), preferred_element_type=jnp.float32)
        lower = carry[1] + lax.dot_general(act, grads, (((0,), (0,)), ((), ())), preferred_element_type=jnp.float32)
        return ((upper, lower), None)
    start = (jnp.zeros((D, FF), jnp.float32), jnp.zeros((FF, D), jnp.float32))
    result, unused = lax.scan(step, start, jnp.arange(count, dtype=jnp.int32))
    return (result[0], result[1])
```

```python
import functools

import jax
import jax.numpy as jnp
from jax import lax
from jax.experimental import pallas as pl
from jax.experimental.pallas import tpu as pltpu
from jax.sharding import PartitionSpec as P

MESH = pl.DeviceIdType.MESH
BF = jnp.bfloat16
F32 = jnp.float32
I32 = jnp.int32
NN = (((1,), (0,)), ((), ()))
NT = (((1,), (1,)), ((), ()))


def dot(a, b, dims):
    return lax.dot_general(a, b, dims, preferred_element_type=F32)


def one_hot(mask):
    return jnp.where(mask, 1.0, 0.0).astype(BF)


def flip(a):
    n = a.shape[1]
    eye = one_hot(lax.broadcasted_iota(I32, (n, n), 0) == lax.broadcasted_iota(I32, (n, n), 1))
    return dot(eye, a, NT).astype(BF)


def kernel(
    cfg, rows_ref, owner_ref, slot_ref, xin_ref, up_ref, down_ref, gu_ref, gd_ref,
    gt, codes, rbuf, acc, obuf, a2buf, ubuf, sibx, xs, gs, act, dgelu, pt, cx, full, s1, cy,
    a1_send, a1_recv, c1_send, c1_recv, sx_send, sx_recv, ring_send, ring_recv, sib_send, sib_recv,
    a2_send, a2_recv, cx_send, cx_recv, cy_send, cy_recv,
):
    nx, ny, nz = cfg
    owners = nx * ny
    tok, width = rows_ref.shape
    ng = xin_ref.shape[0]
    hid = up_ref.shape[1]
    share = width // owners
    half = width // 2
    sub = half // 2
    steps = nz // 2
    pair = 2 * ng
    sect = half // share
    tens = ng // 4
    low = (owners // 2) * 16

    dp, ow = lax.axis_index("dp"), lax.axis_index("owner")
    z, c = dp // 2, dp % 2
    px, py = ow // ny, ow % ny
    sibling = (z * 2 + (1 - c), ow)
    onward = (lax.rem(z + 1, nz) * 2 + c, ow)
    back = (lax.rem(z + nz - 1, nz) * 2 + c, ow)

    def remote(src, dst, send, recv, device):
        return pltpu.make_async_remote_copy(
            src_ref=src, dst_ref=dst, send_sem=send, recv_sem=recv, device_id=device, device_id_type=MESH
        )

    def arrived(dst, send, recv):
        remote(dst, dst, send, recv, sibling).wait_recv()

    def gone(src, send, recv):
        remote(src, src, send, recv, sibling).wait_send()

    def nth(t):
        off = jnp.where(t % 2 == 1, (t + 1) // 2, owners - t // 2)
        return lax.rem(ow + off, owners)

    barrier = pltpu.get_barrier_semaphore()

    def greet(device):
        pl.semaphore_signal(barrier, inc=1, device_id=device, device_id_type=MESH)

    def greet_plane(t, _):
        greet((z * 2, nth(t)))
        greet((z * 2 + 1, nth(t)))
        return 0

    lax.fori_loop(1, owners, greet_plane, 0)
    greet(sibling)
    greet(onward)
    greet(back)

    for b in range(width // 256 if width >= 256 else 1):
        w = min(width, 256)
        gt[b * w:(b + 1) * w, :] = flip(rows_ref[:, b * w:(b + 1) * w])
    owner, slot = owner_ref[...], slot_ref[...]
    k = (
        (slot >= tens).astype(I32) + (slot >= 2 * tens).astype(I32) + (slot >= 3 * tens).astype(I32)
    )
    lo = (owner // 2) * 16 + slot - tens * k
    hi = (owner % 2) * 4 + k
    codes[ow] = hi * 1024 + lo

    pl.semaphore_wait(barrier, 2 * (owners - 1) + 3)

    def half_of(ref, which):
        return ref.at[:, pl.ds(pl.multiple_of(which * half, half), half)]

    swap = remote(half_of(xin_ref, 1 - c), sibx, sx_send, sx_recv, sibling)
    swap.start()

    def rows_to(j):
        return remote(
            gt.at[pl.ds(pl.multiple_of(j * share, share), share)], rbuf.at[ow],
            a1_send.at[j], a1_recv.at[ow], (dp, j),
        )

    def codes_to(j):
        return remote(codes.at[ow], codes.at[ow], c1_send.at[j], c1_recv.at[ow], (dp, j))

    def send_rows(t, _):
        j = nth(t)
        codes_to(j).start()
        rows_to(j).start()
        return 0

    lax.fori_loop(1, owners, send_rows, 0)
    rbuf[ow] = gt[pl.ds(pl.multiple_of(ow * share, share), share), :]

    def piece(buf, block, core, h):
        return buf.at[
            pl.ds(pl.multiple_of(block * pair, 16), pair),
            pl.ds(pl.multiple_of(core * half + h * sub, sub), sub),
        ]

    def to_sibling(n, buf, block, h):
        ref = piece(buf, block, c, h)
        return remote(ref, ref, sib_send.at[n, block, h], sib_recv.at[n, block, h], sibling)

    def to_ring(n, buf, block, d, s, h):
        ref = piece(buf, block, c, h)
        return remote(
            ref, ref, ring_send.at[n, d, s, h], ring_recv.at[n, d, s, h], back if d else onward
        )

    def ring_start(n, buf):
        for h in (0, 1):
            for d in (0, 1):
                to_ring(n, buf, z, d, 0, h).start()
        for h in (0, 1):
            to_sibling(n, buf, z, h).start()

    def ring_step(n, buf, s):
        for h in (0, 1):
            for d in (0, 1):
                block = lax.rem(z + s + 1, nz) if d else lax.rem(z + nz - s - 1, nz)
                last = steps - 1 if h == d else steps - 2

                @pl.when(s <= last)
                def _():
                    arrived(piece(buf, block, c, h), ring_send.at[n, d, s, h], ring_recv.at[n, d, s, h])

                    @pl.when(s < last)
                    def _():
                        to_ring(n, buf, block, d, s + 1, h).start()

                    to_sibling(n, buf, block, h).start()

    def sibling_all(n, buf):
        def one(block, _):
            for h in (0, 1):
                arrived(piece(buf, block, 1 - c, h), sib_send.at[n, block, h], sib_recv.at[n, block, h])
            return 0

        lax.fori_loop(0, nz, one, 0)

    def ring_drain(n, buf):
        def one(s, _):
            for h in (0, 1):
                for d in (0, 1):
                    last = steps - 1 if h == d else steps - 2

                    @pl.when(s <= last)
                    def _():
                        gone(piece(buf, z, c, h), ring_send.at[n, d, s, h], ring_recv.at[n, d, s, h])

            return 0

        lax.fori_loop(0, steps, one, 0)

        def two(block, _):
            for h in (0, 1):
                gone(piece(buf, block, c, h), sib_send.at[n, block, h], sib_recv.at[n, block, h])
            return 0

        lax.fori_loop(0, nz, two, 0)

    def put_own(buf, value):
        here = pl.ds(pl.multiple_of(z * pair, 16), pair)
        for core in (0, 1):

            @pl.when(c == core)
            def _():
                buf[here, core * half:(core + 1) * half] = value

    swap.wait_recv()
    for core in (0, 1):

        @pl.when(c == core)
        def _():
            mine = xin_ref[:, core * half:(core + 1) * half].astype(F32)
            other = sibx[...].astype(F32)
            both = (mine, other) if core == 0 else (other, mine)
            xs[pl.ds(pl.multiple_of(z * pair, 16), pair), core * half:(core + 1) * half] = (
                jnp.concatenate(both, axis=0).astype(BF)
            )

    ring_start(0, xs)

    row_low = lax.broadcasted_iota(I32, (low, tok), 0)
    row_high = lax.broadcasted_iota(I32, (8 * share, tok), 0) // share
    acc[...] = jnp.zeros_like(acc)

    def sum_four(g, _):
        for q in range(4):
            t = 4 * g + q
            src = nth(t)

            @pl.when(t > 0)
            def _():
                arrived(codes.at[src], c1_send.at[src], c1_recv.at[src])
                arrived(rbuf.at[src], a1_send.at[src], a1_recv.at[src])

        total = acc[...]
        for q in range(4):
            src = nth(4 * g + q)
            code = codes[src]
            rows = rbuf[src]
            left = one_hot(row_low == code % 1024)
            right = jnp.concatenate([rows] * 8, axis=0) * one_hot(row_high == code // 1024)
            total = total + dot(left, right, NT)
        acc[...] = total
        ring_step(0, xs, g)
        return 0

    lax.fori_loop(0, steps, sum_four, 0)
    obuf[...] = acc[...].astype(BF)

    home = ow // sect
    seat = ow % sect

    def seat_of(core, s):
        return a2buf.at[
            pl.ds(pl.multiple_of((core * (sect // 4) + s // 4) * 16, 16), 16),
            pl.ds(pl.multiple_of((s % 4) * 128, 128), 128),
        ]

    def sums_of(o):
        return obuf.at[
            pl.ds(pl.multiple_of((o // 2) * 16, 16), 16), pl.ds(pl.multiple_of((o % 2) * 128, 128), 128)
        ]

    def sums_to(o):
        return remote(
            sums_of(o), seat_of(c, seat), a2_send.at[o], a2_recv.at[c * sect + seat], (z * 2 + home, o)
        )

    at_home = home == c

    def send_sums(t, _):
        sums_to(nth(t)).start()
        return 0

    lax.fori_loop(1, owners, send_sums, 0)

    @pl.when(at_home)
    def _():
        keep = pltpu.make_async_copy(sums_of(ow), seat_of(c, seat), a2_send.at[ow])
        keep.start()
        keep.wait()

    @pl.when(jnp.logical_not(at_home))
    def _():
        sums_to(ow).start()

    a = lax.broadcasted_iota(I32, (512, 512), 0)
    b = lax.broadcasted_iota(I32, (512, 512), 1)
    order = one_hot(b == ((a // 32) % 4) * 128 + (a // 128) * 32 + a % 32)
    n = lax.broadcasted_iota(I32, (pair, 128), 0)
    core_of = (n >= ng).astype(I32)
    n = n - ng * core_of
    k = (n >= tens).astype(I32) + (n >= 2 * tens).astype(I32) + (n >= 3 * tens).astype(I32)
    pick = one_hot(
        lax.broadcasted_iota(I32, (pair, 128), 1) == core_of * 64 + k * 16 + n - tens * k
    )
    up_t = flip(up_ref[...])

    def take_sums(u, _):
        core, s = u // sect, u % sect

        @pl.when(jnp.logical_not(jnp.logical_and(core == c, c * sect + s == ow)))
        def _():
            arrived(seat_of(core, s), a2_send.at[0], a2_recv.at[u])

        return 0

    lax.fori_loop(0, owners, take_sums, 0)
    placed = dot(a2buf[...], order, NN).astype(BF)
    parts = sect // 4
    for core in (0, 1):
        for k in range(4):
            for part in range(parts):
                ubuf[(core * 4 + k) * 16:(core * 4 + k + 1) * 16, part * 128:(part + 1) * 128] = placed[
                    (core * parts + part) * 16:(core * parts + part + 1) * 16, k * 128:(k + 1) * 128
                ]
    put_own(gs, dot(pick, ubuf[...], NN).astype(BF))
    ring_start(1, gs)

    sibling_all(0, xs)
    pre = dot(up_t, xs[...], NT)
    scale = 0.7978845608028654
    t = jnp.tanh(scale * (pre + 0.044715 * (pre * pre * pre)))
    act[...] = (pre * (0.5 * (1.0 + t))).astype(BF)
    dgelu[...] = 0.5 * (1.0 + t) + (0.5 * pre) * (1.0 - t * t) * (
        scale * (1.0 + (3.0 * 0.044715) * (pre * pre))
    )

    def next_step(s, _):
        ring_step(1, gs, s)
        return 0

    lax.fori_loop(0, steps, next_step, 0)
    sibling_all(1, gs)

    band = width // nx

    def cx_to(w, xx):
        return remote(
            pt.at[w, pl.ds(pl.multiple_of(xx * band, band), band)], cx.at[w, px],
            cx_send.at[w, xx], cx_recv.at[w, px], (dp, xx * ny + py),
        )

    def cy_to(w, yy):
        return remote(
            s1.at[w, pl.ds(pl.multiple_of(yy * share, share), share)], cy.at[w, py],
            cy_send.at[w, yy], cy_recv.at[w, py], (dp, px * ny + yy),
        )

    def send_partial(w, value):
        step = min(width, 256)
        for b in range(width // step):
            pt[w, b * step:(b + 1) * step, :] = flip(value[:, b * step:(b + 1) * step].astype(BF))
        for i in range(1, nx):
            cx_to(w, lax.rem(px + i, nx)).start()

    def along_x(w):
        total = pt[w, pl.ds(pl.multiple_of(px * band, band), band), :].astype(F32)
        for i in range(1, nx):
            xx = lax.rem(px + i, nx)
            arrived(cx.at[w, xx], cx_send.at[w, xx], cx_recv.at[w, xx])
            total = total + cx[w, xx].astype(F32)
        full[w] = total
        s1[w] = total.astype(BF)
        for i in range(1, ny):
            cy_to(w, lax.rem(py + i, ny)).start()

    def along_y(w):
        total = full[w, pl.ds(pl.multiple_of(py * share, share), share), :]
        for i in range(1, ny):
            yy = lax.rem(py + i, ny)
            arrived(cy.at[w, yy], cy_send.at[w, yy], cy_recv.at[w, yy])
            total = total + cy[w, yy].astype(F32)
        return total

    d_act = dot(down_ref[...], gs[...], NT)
    send_partial(1, dot(act[...], gs[...], NN))
    d_pre = (d_act * dgelu[...]).astype(BF)
    send_partial(0, dot(d_pre, xs[...], NN))
    along_x(1)
    along_x(0)
    down = along_y(1)
    gu_ref[...] = along_y(0)
    wide = jnp.concatenate([down, jnp.zeros((hid - share, hid), F32)], axis=0)
    gd_ref[...] = wide.T[:, :share]

    def drain(t, _):
        j = nth(t)
        rows_to(j).wait_send()
        codes_to(j).wait_send()
        sums_to(j).wait_send()
        return 0

    lax.fori_loop(1, owners, drain, 0)

    @pl.when(jnp.logical_not(at_home))
    def _():
        sums_to(ow).wait_send()

    swap.wait_send()
    ring_drain(0, xs)
    ring_drain(1, gs)
    for w in (0, 1):
        for i in range(1, nx):
            cx_to(w, lax.rem(px + i, nx)).wait_send()
        for i in range(1, ny):
            cy_to(w, lax.rem(py + i, ny)).wait_send()


def on_device(cfg, grad_rows, token_owner, token_slot, ngram_input, up_weight, down_weight):
    nx, ny, nz = cfg
    owners = nx * ny
    tok, width = grad_rows.shape
    ng = ngram_input.shape[0]
    hid = up_weight.shape[1]
    share, half = width // owners, width // 2
    low = (owners // 2) * 16
    total = 2 * nz * ng
    sect = half // share
    dma = pltpu.SemaphoreType.DMA
    vm = pl.BlockSpec(memory_space=pltpu.VMEM)
    return pl.pallas_call(
        functools.partial(kernel, cfg),
        out_shape=(
            jax.ShapeDtypeStruct((share, hid), F32),
            jax.ShapeDtypeStruct((hid, share), F32),
        ),
        in_specs=[vm] * 6,
        out_specs=(vm, vm),
        scratch_shapes=[
            pltpu.VMEM((width, tok), BF),
            pltpu.VMEM((owners, 1, tok), I32),
            pltpu.VMEM((owners, share, tok), BF),
            pltpu.VMEM((low, 8 * share), F32),
            pltpu.VMEM((low, 8 * share), BF),
            pltpu.VMEM((sect // 2 * 16, 512), BF),
            pltpu.VMEM((128, half), BF),
            pltpu.VMEM((ng, half), BF),
            pltpu.VMEM((total, width), BF),
            pltpu.VMEM((total, width), BF),
            pltpu.VMEM((hid, total), BF),
            pltpu.VMEM((hid, total), F32),
            pltpu.VMEM((2, width, hid), BF),
            pltpu.VMEM((2, nx, width // nx, hid), BF),
            pltpu.VMEM((2, width // nx, hid), F32),
            pltpu.VMEM((2, width // nx, hid), BF),
            pltpu.VMEM((2, ny, share, hid), BF),
            dma((owners,)), dma((owners,)),
            dma((owners,)), dma((owners,)),
            dma, dma,
            dma((2, 2, nz // 2, 2)), dma((2, 2, nz // 2, 2)),
            dma((2, nz, 2)), dma((2, nz, 2)),
            dma((owners,)), dma((owners,)),
            dma((2, nx)), dma((2, nx)),
            dma((2, ny)), dma((2, ny)),
        ],
        compiler_params=pltpu.CompilerParams(
            collective_id=0, has_side_effects=True, vmem_limit_bytes=48 * 1024 * 1024
        ),
        name="ngram_backward",
    )(
        grad_rows, token_owner.reshape(1, tok), token_slot.reshape(1, tok),
        ngram_input, up_weight, down_weight,
    )


def solution(mesh):
    owners, dp = mesh.shape["owner"], mesh.shape["dp"]
    nx = 4 if owners == 32 else 2
    cfg = (nx, owners // nx, dp // 2)
    in_specs = (
        P(("dp", "owner"), None),
        P(("dp", "owner")),
        P(("dp", "owner")),
        P(("dp", "owner"), None),
        P(None, "dp"),
        P("dp", None),
    )
    out_specs = (P("owner", "dp"), P("dp", "owner"))
    return jax.shard_map(
        functools.partial(on_device, cfg), mesh=mesh, in_specs=in_specs, out_specs=out_specs, check_vma=False
    )
```

```python
import functools

import jax
import jax.numpy as jnp
from jax import lax
from jax.experimental import pallas as pl
from jax.experimental.pallas import tpu as pltpu
from jax.sharding import PartitionSpec as P

MESH = pl.DeviceIdType.MESH
BF = jnp.bfloat16
F32 = jnp.float32
I32 = jnp.int32
NN = (((1,), (0,)), ((), ()))
NT = (((1,), (1,)), ((), ()))

PIECES = 4


def dot(a, b, dims):
    return lax.dot_general(a, b, dims, preferred_element_type=F32)


def one_hot(mask):
    return jnp.where(mask, 1.0, 0.0).astype(BF)


def flip(a):
    n = a.shape[1]
    eye = one_hot(lax.broadcasted_iota(I32, (n, n), 0) == lax.broadcasted_iota(I32, (n, n), 1))
    return dot(eye, a, NT).astype(BF)


def offsets(owners):
    out = [0]
    for k in range(1, owners // 2):
        out += [k, owners - k]
    return out + [owners // 2]


def kernel(
    cfg, rows_hbm, owner_hbm, slot_hbm, xin_hbm, up_hbm, down_hbm, gu_ref, gd_ref,
    rows_ref, owner_ref, slot_ref, xin_ref, up_ref, down_ref,
    gt, codes, rbuf, acc, obuf, a2buf, ubuf, sums, sibx, sibg, xs, gs, act, dgelu, d_act, pt, cx, full, s1, cy,
    in_sem, a1_send, a1_recv, c1_send, c1_recv, sx_send, sx_recv, sg_send, sg_recv, ring_send, ring_recv, sib_send, sib_recv,
    a2_send, a2_recv, cx_send, cx_recv, cy_send, cy_recv,
):
    nx, ny, nz = cfg
    owners = nx * ny
    tok, width = rows_ref.shape
    ng = xin_ref.shape[0]
    share = width // owners
    half = width // 2
    sub = half // PIECES
    steps = nz // 2
    pair = 2 * ng
    tens = ng // 4
    low = (owners // 2) * 16
    offs = offsets(owners)
    groups = owners // 8

    dp, ow = lax.axis_index("dp"), lax.axis_index("owner")
    z, c = dp // 2, dp % 2
    sibling = (z * 2 + (1 - c), ow)

    def plane(t):
        return lax.rem(ow + offs[t], owners)

    def along(k):
        return (lax.rem(z + k + nz, nz) * 2 + c, ow)

    fetch = [
        pltpu.make_async_copy(a, b, in_sem.at[i])
        for i, (a, b) in enumerate((
            (rows_hbm, rows_ref), (owner_hbm, owner_ref), (slot_hbm, slot_ref),
            (xin_hbm, xin_ref), (up_hbm, up_ref), (down_hbm, down_ref),
        ))
    ]
    for copy in fetch:
        copy.start()

    barrier = pltpu.get_barrier_semaphore()

    def greet(device):
        pl.semaphore_signal(barrier, inc=1, device_id=device, device_id_type=MESH)

    greet(sibling)
    greet(along(1))
    greet(along(-1))
    for t in range(1, owners):
        greet((dp, plane(t)))

    def remote(src, dst, send, recv, device):
        return pltpu.make_async_remote_copy(
            src_ref=src, dst_ref=dst, send_sem=send, recv_sem=recv, device_id=device, device_id_type=MESH
        )

    def arrived(dst, recv):
        remote(dst, dst, recv, recv, sibling).wait_recv()

    def gone(src, send):
        remote(src, src, send, send, sibling).wait_send()

    fetch[1].wait()
    fetch[2].wait()
    owner, slot = owner_ref[...], slot_ref[...]
    k = (
        (slot >= tens).astype(I32) + (slot >= 2 * tens).astype(I32) + (slot >= 3 * tens).astype(I32)
    )
    lo = (owner >> 1) * 16 + slot - tens * k
    hi = (owner & 1) * 4 + k
    codes[0] = hi * 1024 + lo
    fetch[0].wait()
    wide = min(width, 256)
    for b in range(width // wide):
        gt[b * wide:(b + 1) * wide, :] = flip(rows_ref[:, b * wide:(b + 1) * wide])
    fetch[3].wait()

    pl.semaphore_wait(barrier, owners + 2)

    def swap_of(ref, other, send, recv):
        return remote(
            ref.at[:, pl.ds(pl.multiple_of((1 - c) * half, half), half)], other, send, recv, sibling
        )

    swap = swap_of(xin_ref, sibx, sx_send, sx_recv)
    swap.start()
    for t in range(1, owners):
        j = plane(t)
        remote(codes.at[0], codes.at[t], c1_send, c1_recv, (dp, j)).start()
        remote(
            gt.at[pl.ds(pl.multiple_of(j * share, share), share)], rbuf.at[t],
            a1_send, a1_recv.at[t // 8], (dp, j),
        ).start()
    rbuf[0] = gt[pl.ds(pl.multiple_of(ow * share, share), share), :]

    def spot(d, dist):
        return 0 if dist == 0 else 2 * steps - 1 if dist == steps else 2 * dist - 1 + d

    def piece(buf, at, h):
        return buf.at[
            pl.ds(at * pair, pair), pl.ds(pl.multiple_of(c * half + h * sub, sub), sub)
        ]

    def stretch(buf, at, first, count):
        return buf.at[
            pl.ds(at * pair, pair), pl.ds(pl.multiple_of(c * half + first * sub, sub), count * sub)
        ]

    def pieces_of(d, dist):
        return range(PIECES) if dist < steps else range(d * PIECES // 2, (d + 1) * PIECES // 2)

    def forward(n, buf, d, dist, h):
        if dist < steps and h in pieces_of(d, dist + 1):
            remote(
                piece(buf, spot(d, dist), h), piece(buf, spot(d, dist + 1), h),
                ring_send.at[n], ring_recv.at[n, d, dist, h], along(-1 if d else 1),
            ).start()

    def share_core(n, buf, d, dist):
        hs = pieces_of(d, dist)
        ref = stretch(buf, spot(d, dist), hs[0], len(hs))
        part = spot(d, dist) // steps
        remote(ref, ref, sib_send.at[n], sib_recv.at[n, part], sibling).start()

    def ring_start(n, buf):
        for h in range(PIECES):
            for d in (0, 1):
                forward(n, buf, d, 0, h)
        share_core(n, buf, 0, 0)

    def ring_step(n, buf, dist):
        for h in range(PIECES):
            for d in (0, 1):
                if h in pieces_of(d, dist):
                    arrived(piece(buf, spot(d, dist), h), ring_recv.at[n, d, dist - 1, h])
                    forward(n, buf, d, dist, h)
        for d in (0, 1):
            share_core(n, buf, d, dist)

    def sibling_part(n, buf, part):
        arrived(buf.at[pl.ds(part * steps * pair, steps * pair), pl.ds(0, half)], sib_recv.at[n, part])

    def ring_drain(n, buf):
        gone(buf.at[pl.ds(0, (2 * steps - 1) * pair), pl.ds(0, half)], ring_send.at[n])
        gone(buf.at[:, pl.ds(0, half)], sib_send.at[n])

    def put_own(buf, ref, other):
        for core in (0, 1):

            @pl.when(c == core)
            def _():
                both = [ref[:, core * half:(core + 1) * half].astype(F32), other[...].astype(F32)]
                both = both if core == 0 else both[::-1]
                buf[0:pair, core * half:(core + 1) * half] = jnp.concatenate(both, axis=0).astype(BF)

    swap.wait_recv()
    put_own(xs, xin_ref, sibx)
    ring_start(0, xs)

    a = lax.broadcasted_iota(I32, (512, 512), 0)
    b = lax.broadcasted_iota(I32, (512, 512), 1)
    order = one_hot(b == ((a >> 5) & 3) * 128 + (a >> 7) * 32 + (a & 31))
    n = lax.broadcasted_iota(I32, (ng, 64), 0)
    k = (n >= tens).astype(I32) + (n >= 2 * tens).astype(I32) + (n >= 3 * tens).astype(I32)
    pick = one_hot(lax.broadcasted_iota(I32, (ng, 64), 1) == k * 16 + n - tens * k)

    row_low = lax.broadcasted_iota(I32, (low, tok), 0).astype(BF)
    row_high = (lax.broadcasted_iota(I32, (8 * share, tok), 0) >> (share.bit_length() - 1)).astype(BF)
    one, zero = jnp.ones((), BF), jnp.zeros((), BF)
    acc[...] = jnp.zeros_like(acc)

    def sum_two(i, _):
        total = acc[...]
        for q in (0, 1):
            code = codes[2 * i + q]
            rows = rbuf[2 * i + q]
            left = jnp.where(row_low == (code & 1023).astype(F32).astype(BF), one, zero)
            right = jnp.where(
                row_high == (code >> 10).astype(F32).astype(BF), jnp.concatenate([rows] * 8, axis=0), zero
            )
            total = total + dot(left, right, NT)
        acc[...] = total
        return 0

    todo = list(range(1, steps + 1))

    def inputs_on(count):
        for _ in range(min(count, len(todo))):
            ring_step(0, xs, todo.pop(0))

    inputs_on(3)
    arrived(codes.at[pl.ds(1, owners - 1)], c1_recv)
    for g in range(groups):
        first = 1 if g == 0 else 0
        arrived(rbuf.at[pl.ds(8 * g + first, 8 - first)], a1_recv.at[g])
        lax.fori_loop(4 * g, 4 * g + 4, sum_two, 0)
        if g == 0:
            inputs_on(1)
    obuf[...] = acc[...].astype(BF)

    place = a2buf.at[
        pl.ds(pl.multiple_of((ow // 4) * 16, 16), 16), pl.ds(pl.multiple_of((ow % 4) * 128, 128), 128)
    ]

    def sums_of(o):
        return obuf.at[
            pl.ds(pl.multiple_of((o // 2) * 16, 16), 16), pl.ds(pl.multiple_of((o % 2) * 128, 128), 128)
        ]

    for t in range(1, owners):
        o = plane(t)
        remote(sums_of(o), place, a2_send, a2_recv, (dp, o)).start()
    pltpu.make_async_copy(sums_of(ow), place, a2_recv).start()
    fetch[4].wait()
    fetch[5].wait()
    up_t = flip(up_ref[...])
    inputs_on(2)
    arrived(a2buf, a2_recv)
    placed = dot(a2buf[...], order, NN).astype(BF)
    for k in range(4):
        for part in range(owners // 4):
            ubuf[k * 16:(k + 1) * 16, part * 128:(part + 1) * 128] = placed[
                part * 16:(part + 1) * 16, k * 128:(k + 1) * 128
            ]
    sums[...] = dot(pick, ubuf[...], NN).astype(BF)
    swap_sums = swap_of(sums, sibg, sg_send, sg_recv)
    swap_sums.start()
    swap_sums.wait_recv()
    put_own(gs, sums, sibg)
    ring_start(1, gs)

    chunk = xs.shape[0] // 2

    def hidden(i):
        at = slice(i * chunk, (i + 1) * chunk)
        pre = dot(up_t, xs[at, :], NT)
        scale = 0.7978845608028654
        t = jnp.tanh(scale * (pre + 0.044715 * (pre * pre * pre)))
        act[:, at] = (pre * (0.5 * (1.0 + t))).astype(BF)
        dgelu[:, at] = 0.5 * (1.0 + t) + (0.5 * pre) * (1.0 - t * t) * (
            scale * (1.0 + (3.0 * 0.044715) * (pre * pre))
        )

    def grads(i):
        at = slice(i * chunk, (i + 1) * chunk)
        d_act[:, at] = dot(down_ref[...], gs[at, :], NT)

    for dist in range(1, steps + 1):
        inputs_on(1)
        ring_step(1, gs, dist)
        if not todo:
            if dist >= steps // 2 and dist < steps // 2 + 2:
                i = dist - steps // 2
                sibling_part(0, xs, i)
                hidden(i)
            if dist == steps - 1:
                sibling_part(1, gs, 0)
                grads(0)
    sibling_part(1, gs, 1)

    band = width // nx
    px, py = ow // ny, ow % ny

    def send_partial(w, value):
        for b in range(width // wide):
            pt[w, b * wide:(b + 1) * wide, :] = flip(value[:, b * wide:(b + 1) * wide].astype(BF))
        for i in range(1, nx):
            xx = lax.rem(px + i, nx)
            remote(
                pt.at[w, pl.ds(pl.multiple_of(xx * band, band), band)], cx.at[w, i - 1],
                cx_send.at[w], cx_recv.at[w], (dp, xx * ny + py),
            ).start()

    def along_x(w):
        arrived(cx.at[w], cx_recv.at[w])
        total = pt[w, pl.ds(pl.multiple_of(px * band, band), band), :].astype(F32)
        for i in range(1, nx):
            total = total + cx[w, i - 1].astype(F32)
        full[w] = total
        s1[w] = total.astype(BF)
        for i in range(1, ny):
            yy = lax.rem(py + i, ny)
            remote(
                s1.at[w, pl.ds(pl.multiple_of(yy * share, share), share)], cy.at[w, i - 1],
                cy_send.at[w], cy_recv.at[w], (dp, px * ny + yy),
            ).start()

    def along_y(w):
        arrived(cy.at[w], cy_recv.at[w])
        total = full[w, pl.ds(pl.multiple_of(py * share, share), share), :]
        for i in range(1, ny):
            total = total + cy[w, i - 1].astype(F32)
        return total

    send_partial(1, dot(act[...], gs[...], NN))
    grads(1)
    send_partial(0, dot((d_act[...] * dgelu[...]).astype(BF), xs[...], NN))
    along_x(1)
    along_x(0)
    gd_ref[...] = along_y(1)
    gu_ref[...] = along_y(0)

    gone(codes.at[pl.ds(1, owners - 1)], c1_send)
    gone(gt.at[pl.ds(0, (owners - 1) * share)], a1_send)
    gone(gt.at[pl.ds(0, (owners - 1) * 16), pl.ds(0, 128)], a2_send)

    swap.wait_send()
    swap_sums.wait_send()
    ring_drain(0, xs)
    ring_drain(1, gs)
    for w in (0, 1):
        gone(cx.at[w], cx_send.at[w])
        gone(cy.at[w], cy_send.at[w])


def on_device(cfg, grad_rows, token_owner, token_slot, ngram_input, up_weight, down_weight):
    nx, ny, nz = cfg
    owners = nx * ny
    tok, width = grad_rows.shape
    ng = ngram_input.shape[0]
    hid = up_weight.shape[1]
    share, half = width // owners, width // 2
    low = (owners // 2) * 16
    total = 2 * nz * ng
    dma = pltpu.SemaphoreType.DMA
    vm = pl.BlockSpec(memory_space=pltpu.VMEM)
    far = pl.BlockSpec(memory_space=pltpu.HBM)
    up, down = pl.pallas_call(
        functools.partial(kernel, cfg),
        out_shape=(
            jax.ShapeDtypeStruct((share, hid), F32),
            jax.ShapeDtypeStruct((share, hid), F32),
        ),
        in_specs=[far] * 6,
        out_specs=(vm, vm),
        scratch_shapes=[
            pltpu.VMEM((tok, width), BF),
            pltpu.VMEM((1, tok), I32),
            pltpu.VMEM((1, tok), I32),
            pltpu.VMEM((ng, width), BF),
            pltpu.VMEM((width, hid), BF),
            pltpu.VMEM((hid, width), BF),
            pltpu.VMEM((width, tok), BF),
            pltpu.VMEM((owners, 1, tok), I32),
            pltpu.VMEM((owners, share, tok), BF),
            pltpu.VMEM((low, 8 * share), F32),
            pltpu.VMEM((low, 8 * share), BF),
            pltpu.VMEM((owners // 4 * 16, 512), BF),
            pltpu.VMEM((64, width), BF),
            pltpu.VMEM((ng, width), BF),
            pltpu.VMEM((ng, half), BF),
            pltpu.VMEM((ng, half), BF),
            pltpu.VMEM((total, width), BF),
            pltpu.VMEM((total, width), BF),
            pltpu.VMEM((hid, total), BF),
            pltpu.VMEM((hid, total), F32),
            pltpu.VMEM((hid, total), F32),
            pltpu.VMEM((2, width, hid), BF),
            pltpu.VMEM((2, nx - 1, width // nx, hid), BF),
            pltpu.VMEM((2, width // nx, hid), F32),
            pltpu.VMEM((2, width // nx, hid), BF),
            pltpu.VMEM((2, ny - 1, share, hid), BF),
            dma((6,)),
            dma, dma((owners // 8,)),
            dma, dma,
            dma, dma, dma, dma,
            dma((2,)), dma((2, 2, nz // 2, PIECES)),
            dma((2,)), dma((2, 2)),
            dma, dma,
            dma((2,)), dma((2,)),
            dma((2,)), dma((2,)),
        ],
        compiler_params=pltpu.CompilerParams(
            collective_id=0, has_side_effects=True, vmem_limit_bytes=56 * 1024 * 1024
        ),
        name="ngram_backward",
    )(
        grad_rows, token_owner.reshape(1, tok), token_slot.reshape(1, tok),
        ngram_input, up_weight, down_weight,
    )
    return up, down.T


def solution(mesh):
    owners, dp = mesh.shape["owner"], mesh.shape["dp"]
    nx = 4 if owners == 32 else 2
    cfg = (nx, owners // nx, dp // 2)
    in_specs = (
        P(("dp", "owner"), None),
        P(("dp", "owner")),
        P(("dp", "owner")),
        P(("dp", "owner"), None),
        P(None, "dp"),
        P("dp", None),
    )
    out_specs = (P("owner", "dp"), P("dp", "owner"))
    return jax.shard_map(
        functools.partial(on_device, cfg), mesh=mesh, in_specs=in_specs, out_specs=out_specs, check_vma=False
    )
```

```python
import functools

import jax
import jax.numpy as jnp
from jax import lax
from jax.experimental import pallas as pl
from jax.experimental.pallas import tpu as pltpu
from jax.sharding import PartitionSpec as P

MESH = pl.DeviceIdType.MESH
BF = jnp.bfloat16
F32 = jnp.float32
I32 = jnp.int32
NN = (((1,), (0,)), ((), ()))
NT = (((1,), (1,)), ((), ()))

PIECES = 4


def dot(a, b, dims):
    return lax.dot_general(a, b, dims, preferred_element_type=F32)


def one_hot(mask):
    return jnp.where(mask, 1.0, 0.0).astype(BF)


def flip(a):
    n = a.shape[1]
    eye = one_hot(lax.broadcasted_iota(I32, (n, n), 0) == lax.broadcasted_iota(I32, (n, n), 1))
    return dot(eye, a, NT).astype(BF)


def offsets(owners):
    out = [0]
    for k in range(1, owners // 2):
        out += [k, owners - k]
    return out + [owners // 2]


def kernel(
    cfg, rows_hbm, owner_hbm, slot_hbm, xin_hbm, up_hbm, down_hbm, gu_ref, gd_ref,
    rows_ref, owner_ref, slot_ref, xin_ref, up_ref, down_ref,
    gt, codes, rbuf, acc, obuf, a2buf, ubuf, sums, sibx, sibg, xs, gs, act, dgelu, d_act, pt, cx, full, s1, cy,
    in_sem, a1_send, a1_recv, c1_send, c1_recv, sx_send, sx_recv, sg_send, sg_recv, ring_send, ring_recv, sib_send, sib_recv,
    a2_send, a2_recv, cx_send, cx_recv, cy_send, cy_recv,
):
    nx, ny, nz = cfg
    owners = nx * ny
    tok, width = rows_ref.shape
    ng = xin_ref.shape[0]
    share = width // owners
    half = width // 2
    sub = width // PIECES
    steps = nz // 2
    pair = 2 * ng
    tens = ng // 4
    low = (owners // 2) * 16
    offs = offsets(owners)
    groups = owners // 8

    dp, ow = lax.axis_index("dp"), lax.axis_index("owner")
    z, c = dp // 2, dp % 2
    sibling = (z * 2 + (1 - c), ow)

    def plane(t):
        return lax.rem(ow + offs[t], owners)

    def along(k):
        return (lax.rem(z + k + nz, nz) * 2 + c, ow)

    fetch = [
        pltpu.make_async_copy(a, b, in_sem.at[i])
        for i, (a, b) in enumerate((
            (rows_hbm, rows_ref), (owner_hbm, owner_ref), (slot_hbm, slot_ref),
            (xin_hbm, xin_ref), (up_hbm, up_ref), (down_hbm, down_ref),
        ))
    ]
    for copy in fetch:
        copy.start()

    barrier = pltpu.get_barrier_semaphore()

    def greet(device):
        pl.semaphore_signal(barrier, inc=1, device_id=device, device_id_type=MESH)

    greet(sibling)
    greet(along(1))
    greet(along(-1))
    for t in range(1, owners):
        greet((dp, plane(t)))

    def remote(src, dst, send, recv, device):
        return pltpu.make_async_remote_copy(
            src_ref=src, dst_ref=dst, send_sem=send, recv_sem=recv, device_id=device, device_id_type=MESH
        )

    def arrived(dst, recv):
        remote(dst, dst, recv, recv, sibling).wait_recv()

    def gone(src, send):
        remote(src, src, send, send, sibling).wait_send()

    fetch[1].wait()
    fetch[2].wait()
    owner, slot = owner_ref[...], slot_ref[...]
    k = (
        (slot >= tens).astype(I32) + (slot >= 2 * tens).astype(I32) + (slot >= 3 * tens).astype(I32)
    )
    lo = (owner >> 1) * 16 + slot - tens * k
    hi = (owner & 1) * 4 + k
    codes[0] = hi * 1024 + lo
    fetch[0].wait()
    wide = min(width, 256)
    for b in range(width // wide):
        gt[b * wide:(b + 1) * wide, :] = flip(rows_ref[:, b * wide:(b + 1) * wide])
    fetch[3].wait()

    pl.semaphore_wait(barrier, owners + 2)

    swap = remote(xin_ref, sibx, sx_send, sx_recv, sibling)
    swap.start()
    for t in range(1, owners):
        j = plane(t)
        remote(codes.at[0], codes.at[t], c1_send, c1_recv, (dp, j)).start()
        remote(
            gt.at[pl.ds(pl.multiple_of(j * share, share), share)], rbuf.at[t],
            a1_send, a1_recv.at[t // 8], (dp, j),
        ).start()
    rbuf[0] = gt[pl.ds(pl.multiple_of(ow * share, share), share), :]

    onward = along(1 - 2 * c)

    def rows_at(dist):
        at = 0 if dist == 0 else 2 * steps - 1 if dist == steps else 2 * dist - 1 + c
        return pl.ds(pl.multiple_of(at * pair, 16), pair)

    def piece(buf, dist, h):
        first = lax.rem(h * sub + c * half, width)
        return buf.at[rows_at(dist), pl.ds(pl.multiple_of(first, sub), sub)]

    def pieces_of(dist):
        return range(PIECES if dist < steps else PIECES // 2)

    def forward(n, buf, dist, h):
        if dist < steps and h in pieces_of(dist + 1):
            remote(
                piece(buf, dist, h), piece(buf, dist + 1, h),
                ring_send.at[n], ring_recv.at[n, dist, h], onward,
            ).start()

    def ring_start(n, buf):
        for h in range(PIECES):
            forward(n, buf, 0, h)

    def ring_step(n, buf, dist):
        for h in pieces_of(dist):
            arrived(piece(buf, dist, h), ring_recv.at[n, dist - 1, h])
            forward(n, buf, dist, h)
        cols = pl.ds(0, width) if dist < steps else pl.ds(pl.multiple_of(c * half, half), half)
        ref = buf.at[rows_at(dist), cols]
        remote(
            ref, ref, sib_send.at[n], sib_recv.at[n, 0 if dist <= steps // 2 else 1], sibling
        ).start()

    def sibling_part(n, buf, part):
        if part == 0:
            arrived(buf.at[pl.ds(0, steps // 2 * pair)], sib_recv.at[n, 0])
        else:
            arrived(buf.at[pl.ds(0, (steps - 1) * pair), pl.ds(0, half)], sib_recv.at[n, 1])

    def ring_drain(n, buf):
        sent = buf.at[pl.ds(0, (2 * steps - 1) * pair), pl.ds(0, half)]
        gone(sent, ring_send.at[n])
        gone(sent, sib_send.at[n])

    def put_own(buf, ref, other):
        for core in (0, 1):

            @pl.when(c == core)
            def _():
                both = [ref[...].astype(F32), other[...].astype(F32)]
                both = both if core == 0 else both[::-1]
                buf[0:pair, :] = jnp.concatenate(both, axis=0).astype(BF)

    swap.wait_recv()
    put_own(xs, xin_ref, sibx)
    ring_start(0, xs)

    a = lax.broadcasted_iota(I32, (512, 512), 0)
    b = lax.broadcasted_iota(I32, (512, 512), 1)
    order = one_hot(b == ((a >> 5) & 3) * 128 + (a >> 7) * 32 + (a & 31))
    n = lax.broadcasted_iota(I32, (ng, 64), 0)
    k = (n >= tens).astype(I32) + (n >= 2 * tens).astype(I32) + (n >= 3 * tens).astype(I32)
    pick = one_hot(lax.broadcasted_iota(I32, (ng, 64), 1) == k * 16 + n - tens * k)

    row_low = lax.broadcasted_iota(I32, (low, tok), 0).astype(BF)
    row_high = (lax.broadcasted_iota(I32, (8 * share, tok), 0) >> (share.bit_length() - 1)).astype(BF)
    one, zero = jnp.ones((), BF), jnp.zeros((), BF)

    def sum_group(g):
        left, right = [], []
        for t in range(8 * g, 8 * g + 8):
            code = codes[t]
            left.append(jnp.where(row_low == (code & 1023).astype(F32).astype(BF), one, zero))
            right.append(jnp.where(
                row_high == (code >> 10).astype(F32).astype(BF), jnp.concatenate([rbuf[t]] * 8, axis=0), zero
            ))
        total = dot(jnp.concatenate(left, axis=1), jnp.concatenate(right, axis=1), NT)
        acc[...] = total if g == 0 else acc[...] + total

    todo = list(range(1, steps + 1))

    def inputs_on(count):
        for _ in range(min(count, len(todo))):
            ring_step(0, xs, todo.pop(0))

    inputs_on(3)
    arrived(codes.at[pl.ds(1, owners - 1)], c1_recv)
    for g in range(groups):
        first = 1 if g == 0 else 0
        arrived(rbuf.at[pl.ds(8 * g + first, 8 - first)], a1_recv.at[g])
        sum_group(g)
        if g == 0:
            inputs_on(1)
    obuf[...] = acc[...].astype(BF)

    place = a2buf.at[
        pl.ds(pl.multiple_of((ow // 4) * 16, 16), 16), pl.ds(pl.multiple_of((ow % 4) * 128, 128), 128)
    ]

    def sums_of(o):
        return obuf.at[
            pl.ds(pl.multiple_of((o // 2) * 16, 16), 16), pl.ds(pl.multiple_of((o % 2) * 128, 128), 128)
        ]

    for t in range(1, owners):
        o = plane(t)
        remote(sums_of(o), place, a2_send, a2_recv, (dp, o)).start()
    pltpu.make_async_copy(sums_of(ow), place, a2_recv).start()
    fetch[4].wait()
    fetch[5].wait()
    up_t = flip(up_ref[...])
    inputs_on(2)
    arrived(a2buf, a2_recv)
    placed = dot(a2buf[...], order, NN).astype(BF)
    for k in range(4):
        for part in range(owners // 4):
            ubuf[k * 16:(k + 1) * 16, part * 128:(part + 1) * 128] = placed[
                part * 16:(part + 1) * 16, k * 128:(k + 1) * 128
            ]
    sums[...] = dot(pick, ubuf[...], NN).astype(BF)
    swap_sums = remote(sums, sibg, sg_send, sg_recv, sibling)
    swap_sums.start()
    swap_sums.wait_recv()
    put_own(gs, sums, sibg)
    ring_start(1, gs)

    chunk = xs.shape[0] // 2

    def hidden(i):
        at = slice(i * chunk, (i + 1) * chunk)
        pre = dot(up_t, xs[at, :], NT)
        scale = 0.7978845608028654
        t = jnp.tanh(scale * (pre + 0.044715 * (pre * pre * pre)))
        act[:, at] = (pre * (0.5 * (1.0 + t))).astype(BF)
        dgelu[:, at] = 0.5 * (1.0 + t) + (0.5 * pre) * (1.0 - t * t) * (
            scale * (1.0 + (3.0 * 0.044715) * (pre * pre))
        )

    def grads(i):
        at = slice(i * chunk, (i + 1) * chunk)
        d_act[:, at] = dot(down_ref[...], gs[at, :], NT)

    for dist in range(1, steps + 1):
        inputs_on(1)
        ring_step(1, gs, dist)
        if not todo:
            if dist >= steps // 2 and dist < steps // 2 + 2:
                i = dist - steps // 2
                sibling_part(0, xs, i)
                hidden(i)
            if dist == steps - 1:
                sibling_part(1, gs, 0)
                grads(0)
    sibling_part(1, gs, 1)

    band = width // nx
    px, py = ow // ny, ow % ny

    def send_partial(w, value):
        for b in range(width // wide):
            pt[w, b * wide:(b + 1) * wide, :] = flip(value[:, b * wide:(b + 1) * wide].astype(BF))
        for i in range(1, nx):
            xx = lax.rem(px + i, nx)
            remote(
                pt.at[w, pl.ds(pl.multiple_of(xx * band, band), band)], cx.at[w, i - 1],
                cx_send.at[w], cx_recv.at[w], (dp, xx * ny + py),
            ).start()

    def along_x(w):
        arrived(cx.at[w], cx_recv.at[w])
        total = pt[w, pl.ds(pl.multiple_of(px * band, band), band), :].astype(F32)
        for i in range(1, nx):
            total = total + cx[w, i - 1].astype(F32)
        full[w] = total
        s1[w] = total.astype(BF)
        for i in range(1, ny):
            yy = lax.rem(py + i, ny)
            remote(
                s1.at[w, pl.ds(pl.multiple_of(yy * share, share), share)], cy.at[w, i - 1],
                cy_send.at[w], cy_recv.at[w], (dp, px * ny + yy),
            ).start()

    def along_y(w):
        arrived(cy.at[w], cy_recv.at[w])
        total = full[w, pl.ds(pl.multiple_of(py * share, share), share), :]
        for i in range(1, ny):
            total = total + cy[w, i - 1].astype(F32)
        return total

    send_partial(1, dot(act[...], gs[...], NN))
    grads(1)
    send_partial(0, dot((d_act[...] * dgelu[...]).astype(BF), xs[...], NN))
    along_x(1)
    along_x(0)
    gd_ref[...] = along_y(1)
    gu_ref[...] = along_y(0)

    gone(codes.at[pl.ds(1, owners - 1)], c1_send)
    gone(gt.at[pl.ds(0, (owners - 1) * share)], a1_send)
    gone(gt.at[pl.ds(0, (owners - 1) * 16), pl.ds(0, 128)], a2_send)

    swap.wait_send()
    swap_sums.wait_send()
    ring_drain(0, xs)
    ring_drain(1, gs)
    for w in (0, 1):
        gone(cx.at[w], cx_send.at[w])
        gone(cy.at[w], cy_send.at[w])


def on_device(cfg, grad_rows, token_owner, token_slot, ngram_input, up_weight, down_weight):
    nx, ny, nz = cfg
    owners = nx * ny
    tok, width = grad_rows.shape
    ng = ngram_input.shape[0]
    hid = up_weight.shape[1]
    share, half = width // owners, width // 2
    low = (owners // 2) * 16
    total = 2 * nz * ng
    dma = pltpu.SemaphoreType.DMA
    vm = pl.BlockSpec(memory_space=pltpu.VMEM)
    far = pl.BlockSpec(memory_space=pltpu.HBM)
    up, down = pl.pallas_call(
        functools.partial(kernel, cfg),
        out_shape=(
            jax.ShapeDtypeStruct((share, hid), F32),
            jax.ShapeDtypeStruct((share, hid), F32),
        ),
        in_specs=[far] * 6,
        out_specs=(vm, vm),
        scratch_shapes=[
            pltpu.VMEM((tok, width), BF),
            pltpu.VMEM((1, tok), I32),
            pltpu.VMEM((1, tok), I32),
            pltpu.VMEM((ng, width), BF),
            pltpu.VMEM((width, hid), BF),
            pltpu.VMEM((hid, width), BF),
            pltpu.VMEM((width, tok), BF),
            pltpu.VMEM((owners, 1, tok), I32),
            pltpu.VMEM((owners, share, tok), BF),
            pltpu.VMEM((low, 8 * share), F32),
            pltpu.VMEM((low, 8 * share), BF),
            pltpu.VMEM((owners // 4 * 16, 512), BF),
            pltpu.VMEM((64, width), BF),
            pltpu.VMEM((ng, width), BF),
            pltpu.VMEM((ng, width), BF),
            pltpu.VMEM((ng, width), BF),
            pltpu.VMEM((total, width), BF),
            pltpu.VMEM((total, width), BF),
            pltpu.VMEM((hid, total), BF),
            pltpu.VMEM((hid, total), F32),
            pltpu.VMEM((hid, total), F32),
            pltpu.VMEM((2, width, hid), BF),
            pltpu.VMEM((2, nx - 1, width // nx, hid), BF),
            pltpu.VMEM((2, width // nx, hid), F32),
            pltpu.VMEM((2, width // nx, hid), BF),
            pltpu.VMEM((2, ny - 1, share, hid), BF),
            dma((6,)),
            dma, dma((owners // 8,)),
            dma, dma,
            dma, dma, dma, dma,
            dma((2,)), dma((2, nz // 2, PIECES)),
            dma((2,)), dma((2, 2)),
            dma, dma,
            dma((2,)), dma((2,)),
            dma((2,)), dma((2,)),
        ],
        compiler_params=pltpu.CompilerParams(
            collective_id=0, has_side_effects=True, vmem_limit_bytes=56 * 1024 * 1024
        ),
        name="ngram_backward",
    )(
        grad_rows, token_owner.reshape(1, tok), token_slot.reshape(1, tok),
        ngram_input, up_weight, down_weight,
    )
    return up, down.T


def solution(mesh):
    owners, dp = mesh.shape["owner"], mesh.shape["dp"]
    nx = 4 if owners == 32 else 2
    cfg = (nx, owners // nx, dp // 2)
    in_specs = (
        P(("dp", "owner"), None),
        P(("dp", "owner")),
        P(("dp", "owner")),
        P(("dp", "owner"), None),
        P(None, "dp"),
        P("dp", None),
    )
    out_specs = (P("owner", "dp"), P("dp", "owner"))
    return jax.shard_map(
        functools.partial(on_device, cfg), mesh=mesh, in_specs=in_specs, out_specs=out_specs, check_vma=False
    )
```

```python
import functools

import jax
import jax.numpy as jnp
from jax import lax
from jax.experimental import pallas as pl
from jax.experimental.pallas import tpu as pltpu
from jax.sharding import PartitionSpec as P

MESH = pl.DeviceIdType.MESH
BF = jnp.bfloat16
F32 = jnp.float32
I32 = jnp.int32
NN = (((1,), (0,)), ((), ()))
NT = (((1,), (1,)), ((), ()))

PIECES = 4


def dot(a, b, dims):
    return lax.dot_general(a, b, dims, preferred_element_type=F32)


def one_hot(mask):
    return jnp.where(mask, 1.0, 0.0).astype(BF)


def flip(a):
    n = a.shape[1]
    eye = one_hot(lax.broadcasted_iota(I32, (n, n), 0) == lax.broadcasted_iota(I32, (n, n), 1))
    return dot(eye, a, NT).astype(BF)


def offsets(nx, ny):
    both = [(dx, dy) for dx in range(nx) for dy in range(ny)]
    return sorted(both, key=lambda v: min(v[0], nx - v[0]) + min(v[1], ny - v[1]))


def far_first(n):
    return sorted(range(1, n), key=lambda i: -min(i, n - i))


def kernel(
    cfg, rows_hbm, owner_hbm, slot_hbm, xin_hbm, up_hbm, down_hbm, gu_ref, gd_ref,
    rows_ref, owner_ref, slot_ref, xin_ref, up_ref, down_ref,
    gt, codes, rbuf, acc, obuf, a2buf, ubuf, sums, sibx, sibg, xs, gs, act, dgelu, d_act, pt, cx, full, s1, cy,
    in_sem, a1_send, a1_recv, c1_send, c1_recv, sx_send, sx_recv, sg_send, sg_recv, ring_send, ring_recv, sib_send, sib_recv,
    a2_send, a2_recv, cx_send, cx_recv, cy_send, cy_recv,
):
    nx, ny, nz = cfg
    owners = nx * ny
    tok, width = rows_ref.shape
    ng = xin_ref.shape[0]
    share = width // owners
    half = width // 2
    sub = width // PIECES
    steps = nz // 2
    pair = 2 * ng
    tens = ng // 4
    low = (owners // 2) * 16
    offs = offsets(nx, ny)
    groups = owners // 8

    dp, ow = lax.axis_index("dp"), lax.axis_index("owner")
    z, c = dp // 2, dp % 2
    px, py = ow // ny, ow % ny
    sibling = (z * 2 + (1 - c), ow)

    def plane(t):
        dx, dy = offs[t]
        return lax.rem(px + dx, nx) * ny + lax.rem(py + dy, ny)

    def along(k):
        return (lax.rem(z + k + nz, nz) * 2 + c, ow)

    fetch = [
        pltpu.make_async_copy(a, b, in_sem.at[i])
        for i, (a, b) in enumerate((
            (rows_hbm, rows_ref), (owner_hbm, owner_ref), (slot_hbm, slot_ref),
            (xin_hbm, xin_ref), (up_hbm, up_ref), (down_hbm, down_ref),
        ))
    ]
    for copy in fetch:
        copy.start()

    barrier = pltpu.get_barrier_semaphore()

    def greet(device):
        pl.semaphore_signal(barrier, inc=1, device_id=device, device_id_type=MESH)

    for t in range(owners - 1, 0, -1):
        greet((dp, plane(t)))
    greet(along(1))
    greet(along(-1))
    greet(sibling)

    def remote(src, dst, send, recv, device):
        return pltpu.make_async_remote_copy(
            src_ref=src, dst_ref=dst, send_sem=send, recv_sem=recv, device_id=device, device_id_type=MESH
        )

    def arrived(dst, recv):
        remote(dst, dst, recv, recv, sibling).wait_recv()

    def gone(src, send):
        remote(src, src, send, send, sibling).wait_send()

    fetch[1].wait()
    fetch[2].wait()
    owner, slot = owner_ref[...], slot_ref[...]
    k = (
        (slot >= tens).astype(I32) + (slot >= 2 * tens).astype(I32) + (slot >= 3 * tens).astype(I32)
    )
    lo = (owner >> 1) * 16 + slot - tens * k
    hi = (owner & 1) * 4 + k
    codes[0] = hi * 1024 + lo
    fetch[0].wait()
    wide = min(width, 256)
    for b in range(width // wide):
        gt[b * wide:(b + 1) * wide, :] = flip(rows_ref[:, b * wide:(b + 1) * wide])
    fetch[3].wait()

    pl.semaphore_wait(barrier, owners + 2)

    swap = remote(xin_ref, sibx, sx_send, sx_recv, sibling)
    swap.start()
    for t in range(owners - 1, 0, -1):
        j = plane(t)
        remote(codes.at[0], codes.at[t], c1_send, c1_recv, (dp, j)).start()
        remote(
            gt.at[pl.ds(pl.multiple_of(j * share, share), share)], rbuf.at[t],
            a1_send, a1_recv.at[t // 8], (dp, j),
        ).start()
    rbuf[0] = gt[pl.ds(pl.multiple_of(ow * share, share), share), :]

    onward = along(1 - 2 * c)

    def rows_at(dist):
        at = 0 if dist == 0 else 2 * steps - 1 if dist == steps else 2 * dist - 1 + c
        return pl.ds(pl.multiple_of(at * pair, 16), pair)

    def piece(buf, dist, h):
        first = lax.rem(h * sub + c * half, width)
        return buf.at[rows_at(dist), pl.ds(pl.multiple_of(first, sub), sub)]

    def pieces_of(dist):
        return range(PIECES if dist < steps else PIECES // 2)

    def forward(n, buf, dist, h):
        if dist < steps and h in pieces_of(dist + 1):
            remote(
                piece(buf, dist, h), piece(buf, dist + 1, h),
                ring_send.at[n], ring_recv.at[n, dist, h], onward,
            ).start()

    def ring_start(n, buf):
        for h in range(PIECES):
            forward(n, buf, 0, h)

    def ring_step(n, buf, dist):
        for h in pieces_of(dist):
            arrived(piece(buf, dist, h), ring_recv.at[n, dist - 1, h])
            forward(n, buf, dist, h)
        cols = pl.ds(0, width) if dist < steps else pl.ds(pl.multiple_of(c * half, half), half)
        ref = buf.at[rows_at(dist), cols]
        remote(
            ref, ref, sib_send.at[n], sib_recv.at[n, 0 if dist <= steps // 2 else 1], sibling
        ).start()

    def sibling_part(n, buf, part):
        if part == 0:
            arrived(buf.at[pl.ds(0, steps // 2 * pair)], sib_recv.at[n, 0])
        else:
            arrived(buf.at[pl.ds(0, (steps - 1) * pair), pl.ds(0, half)], sib_recv.at[n, 1])

    def ring_drain(n, buf):
        sent = buf.at[pl.ds(0, (2 * steps - 1) * pair), pl.ds(0, half)]
        gone(sent, ring_send.at[n])
        gone(sent, sib_send.at[n])

    def put_own(buf, ref, other):
        for core in (0, 1):

            @pl.when(c == core)
            def _():
                both = [ref[...].astype(F32), other[...].astype(F32)]
                both = both if core == 0 else both[::-1]
                buf[0:pair, :] = jnp.concatenate(both, axis=0).astype(BF)

    swap.wait_recv()
    put_own(xs, xin_ref, sibx)
    ring_start(0, xs)

    a = lax.broadcasted_iota(I32, (512, 512), 0)
    b = lax.broadcasted_iota(I32, (512, 512), 1)
    order = one_hot(b == ((a >> 5) & 3) * 128 + (a >> 7) * 32 + (a & 31))
    n = lax.broadcasted_iota(I32, (ng, 64), 0)
    k = (n >= tens).astype(I32) + (n >= 2 * tens).astype(I32) + (n >= 3 * tens).astype(I32)
    pick = one_hot(lax.broadcasted_iota(I32, (ng, 64), 1) == k * 16 + n - tens * k)

    row_low = lax.broadcasted_iota(I32, (low, tok), 0).astype(BF)
    row_high = (lax.broadcasted_iota(I32, (8 * share, tok), 0) >> (share.bit_length() - 1)).astype(BF)
    one, zero = jnp.ones((), BF), jnp.zeros((), BF)

    def sum_group(g):
        left, right = [], []
        for t in range(8 * g, 8 * g + 8):
            code = codes[t]
            left.append(jnp.where(row_low == (code & 1023).astype(F32).astype(BF), one, zero))
            right.append(jnp.where(
                row_high == (code >> 10).astype(F32).astype(BF), jnp.concatenate([rbuf[t]] * 8, axis=0), zero
            ))
        total = dot(jnp.concatenate(left, axis=1), jnp.concatenate(right, axis=1), NT)
        acc[...] = total if g == groups - 1 else acc[...] + total

    todo = list(range(1, steps + 1))

    def inputs_on(count):
        for _ in range(min(count, len(todo))):
            ring_step(0, xs, todo.pop(0))

    inputs_on(3)
    arrived(codes.at[pl.ds(1, owners - 1)], c1_recv)
    for g in range(groups - 1, -1, -1):
        first = 1 if g == 0 else 0
        arrived(rbuf.at[pl.ds(8 * g + first, 8 - first)], a1_recv.at[g])
        sum_group(g)
        if g == groups - 1:
            inputs_on(1)
    obuf[...] = acc[...].astype(BF)

    place = a2buf.at[
        pl.ds(pl.multiple_of((ow // 4) * 16, 16), 16), pl.ds(pl.multiple_of((ow % 4) * 128, 128), 128)
    ]

    def sums_of(o):
        return obuf.at[
            pl.ds(pl.multiple_of((o // 2) * 16, 16), 16), pl.ds(pl.multiple_of((o % 2) * 128, 128), 128)
        ]

    for t in range(owners - 1, 0, -1):
        o = plane(t)
        remote(sums_of(o), place, a2_send, a2_recv, (dp, o)).start()
    pltpu.make_async_copy(sums_of(ow), place, a2_recv).start()
    fetch[4].wait()
    fetch[5].wait()
    up_t = flip(up_ref[...])
    inputs_on(2)
    arrived(a2buf, a2_recv)
    placed = dot(a2buf[...], order, NN).astype(BF)
    for k in range(4):
        for part in range(owners // 4):
            ubuf[k * 16:(k + 1) * 16, part * 128:(part + 1) * 128] = placed[
                part * 16:(part + 1) * 16, k * 128:(k + 1) * 128
            ]
    sums[...] = dot(pick, ubuf[...], NN).astype(BF)
    swap_sums = remote(sums, sibg, sg_send, sg_recv, sibling)
    swap_sums.start()
    swap_sums.wait_recv()
    put_own(gs, sums, sibg)
    ring_start(1, gs)

    chunk = xs.shape[0] // 2

    def hidden(i):
        at = slice(i * chunk, (i + 1) * chunk)
        pre = dot(up_t, xs[at, :], NT)
        scale = 0.7978845608028654
        t = jnp.tanh(scale * (pre + 0.044715 * (pre * pre * pre)))
        act[:, at] = (pre * (0.5 * (1.0 + t))).astype(BF)
        dgelu[:, at] = 0.5 * (1.0 + t) + (0.5 * pre) * (1.0 - t * t) * (
            scale * (1.0 + (3.0 * 0.044715) * (pre * pre))
        )

    def grads(i):
        at = slice(i * chunk, (i + 1) * chunk)
        d_act[:, at] = dot(down_ref[...], gs[at, :], NT)

    for dist in range(1, steps + 1):
        inputs_on(1)
        ring_step(1, gs, dist)
        if not todo:
            if dist >= steps // 2 and dist < steps // 2 + 2:
                i = dist - steps // 2
                sibling_part(0, xs, i)
                hidden(i)
            if dist == steps - 1:
                sibling_part(1, gs, 0)
                grads(0)
    sibling_part(1, gs, 1)

    band = width // nx

    def send_partial(w, value):
        for b in range(width // wide):
            pt[w, b * wide:(b + 1) * wide, :] = flip(value[:, b * wide:(b + 1) * wide].astype(BF))
        for i in far_first(nx):
            xx = lax.rem(px + i, nx)
            remote(
                pt.at[w, pl.ds(pl.multiple_of(xx * band, band), band)], cx.at[w, i - 1],
                cx_send.at[w], cx_recv.at[w], (dp, xx * ny + py),
            ).start()

    def along_x(w):
        arrived(cx.at[w], cx_recv.at[w])
        total = pt[w, pl.ds(pl.multiple_of(px * band, band), band), :].astype(F32)
        for i in range(1, nx):
            total = total + cx[w, i - 1].astype(F32)
        full[w] = total
        s1[w] = total.astype(BF)
        for i in far_first(ny):
            yy = lax.rem(py + i, ny)
            remote(
                s1.at[w, pl.ds(pl.multiple_of(yy * share, share), share)], cy.at[w, i - 1],
                cy_send.at[w], cy_recv.at[w], (dp, px * ny + yy),
            ).start()

    def along_y(w):
        arrived(cy.at[w], cy_recv.at[w])
        total = full[w, pl.ds(pl.multiple_of(py * share, share), share), :]
        for i in range(1, ny):
            total = total + cy[w, i - 1].astype(F32)
        return total

    send_partial(1, dot(act[...], gs[...], NN))
    grads(1)
    send_partial(0, dot((d_act[...] * dgelu[...]).astype(BF), xs[...], NN))
    along_x(1)
    along_x(0)
    gd_ref[...] = along_y(1)
    gu_ref[...] = along_y(0)

    gone(codes.at[pl.ds(1, owners - 1)], c1_send)
    gone(gt.at[pl.ds(0, (owners - 1) * share)], a1_send)
    gone(gt.at[pl.ds(0, (owners - 1) * 16), pl.ds(0, 128)], a2_send)

    swap.wait_send()
    swap_sums.wait_send()
    ring_drain(0, xs)
    ring_drain(1, gs)
    for w in (0, 1):
        gone(cx.at[w], cx_send.at[w])
        gone(cy.at[w], cy_send.at[w])


def on_device(cfg, grad_rows, token_owner, token_slot, ngram_input, up_weight, down_weight):
    nx, ny, nz = cfg
    owners = nx * ny
    tok, width = grad_rows.shape
    ng = ngram_input.shape[0]
    hid = up_weight.shape[1]
    share, half = width // owners, width // 2
    low = (owners // 2) * 16
    total = 2 * nz * ng
    dma = pltpu.SemaphoreType.DMA
    vm = pl.BlockSpec(memory_space=pltpu.VMEM)
    far = pl.BlockSpec(memory_space=pltpu.HBM)
    up, down = pl.pallas_call(
        functools.partial(kernel, cfg),
        out_shape=(
            jax.ShapeDtypeStruct((share, hid), F32),
            jax.ShapeDtypeStruct((share, hid), F32),
        ),
        in_specs=[far] * 6,
        out_specs=(vm, vm),
        scratch_shapes=[
            pltpu.VMEM((tok, width), BF),
            pltpu.VMEM((1, tok), I32),
            pltpu.VMEM((1, tok), I32),
            pltpu.VMEM((ng, width), BF),
            pltpu.VMEM((width, hid), BF),
            pltpu.VMEM((hid, width), BF),
            pltpu.VMEM((width, tok), BF),
            pltpu.VMEM((owners, 1, tok), I32),
            pltpu.VMEM((owners, share, tok), BF),
            pltpu.VMEM((low, 8 * share), F32),
            pltpu.VMEM((low, 8 * share), BF),
            pltpu.VMEM((owners // 4 * 16, 512), BF),
            pltpu.VMEM((64, width), BF),
            pltpu.VMEM((ng, width), BF),
            pltpu.VMEM((ng, width), BF),
            pltpu.VMEM((ng, width), BF),
            pltpu.VMEM((total, width), BF),
            pltpu.VMEM((total, width), BF),
            pltpu.VMEM((hid, total), BF),
            pltpu.VMEM((hid, total), F32),
            pltpu.VMEM((hid, total), F32),
            pltpu.VMEM((2, width, hid), BF),
            pltpu.VMEM((2, nx - 1, width // nx, hid), BF),
            pltpu.VMEM((2, width // nx, hid), F32),
            pltpu.VMEM((2, width // nx, hid), BF),
            pltpu.VMEM((2, ny - 1, share, hid), BF),
            dma((6,)),
            dma, dma((owners // 8,)),
            dma, dma,
            dma, dma, dma, dma,
            dma((2,)), dma((2, nz // 2, PIECES)),
            dma((2,)), dma((2, 2)),
            dma, dma,
            dma((2,)), dma((2,)),
            dma((2,)), dma((2,)),
        ],
        compiler_params=pltpu.CompilerParams(
            collective_id=0, has_side_effects=True, vmem_limit_bytes=56 * 1024 * 1024
        ),
        name="ngram_backward",
    )(
        grad_rows, token_owner.reshape(1, tok), token_slot.reshape(1, tok),
        ngram_input, up_weight, down_weight,
    )
    return up, down.T


def solution(mesh):
    owners, dp = mesh.shape["owner"], mesh.shape["dp"]
    nx = 4 if owners == 32 else 2
    cfg = (nx, owners // nx, dp // 2)
    in_specs = (
        P(("dp", "owner"), None),
        P(("dp", "owner")),
        P(("dp", "owner")),
        P(("dp", "owner"), None),
        P(None, "dp"),
        P("dp", None),
    )
    out_specs = (P("owner", "dp"), P("dp", "owner"))
    return jax.shard_map(
        functools.partial(on_device, cfg), mesh=mesh, in_specs=in_specs, out_specs=out_specs, check_vma=False
    )
```
